32 devices in a mesh: row: 4 (over z), col: 8 (over y, x, core).
Axes of the slice: x: 2, y: 2, z: 4, core: 2. Of those that a mesh axis runs over, the one named last changes fastest.
Arguments:
- ancestor: float32 [16384, 16384], P('row', 'col'), may hold values from -6 to 6
- factor: float32 [2, 16384, 512], P(None, ('row', 'col')), may hold values from -0.0625 to 0.0625
- diag_inverse: float32 [2, 512, 512], replicated, may hold values from -6 to 6
- structure: int32 [2, 16], replicated, may hold values from 0 to 31, as said below
Outputs:
- off_diagonal: float32 [2, 16384, 512], P(None, ('row', 'col'))
- diag_block: float32 [2, 512, 512], replicated
The draws below stay inside these ranges and needn't reach their ends.
Inputs may be any that keep to these rules, and one draw needn't show every extreme that they name: `structure`: each row holds 16 distinct tile indices; tile t covers rows t * 512 to t * 512 + 511.
All inputs are finite; a program needn't handle non-finite values.
Results may differ from the reference program's by a relative error of at most 0.0001.
Values sent between devices are 32-bit elements; how exact they have to be, the bound alone decides.
A program may use at most 128 MiB of HBM per device.

```python
import jax
import jax.numpy as jnp
from jax import lax

ORDER = 16384
TILE = 512
WIDTH = 512
LIST = 16


def draw_structure(key, part):
    chosen = []
    for supernode in range(2):
        shuffled = jax.random.permutation(jax.random.fold_in(key, 11 + supernode), ORDER // TILE)
        chosen.append(shuffled[:LIST])
    return jnp.stack(chosen).astype(jnp.int32)


def level_of(stream_key, dims, split, low, top_value):
    def one(position, blocks):
        draws = jax.random.uniform(jax.random.fold_in(jax.random.fold_in(stream_key, 6), position), (blocks,), jnp.float32, low / len(split), top_value / len(split))
        return jnp.repeat(jnp.exp(draws), dims[position] // blocks).reshape((-1,) + (1,) * (len(dims) - position - 1))

    level = one(*split[0])
    for cut in split[1:]:
        level = level * one(*cut)
    return level


def bell_draw(rng, shape, scale, reach, pieces=(), kind=jnp.bfloat16):
    entries = scale * jax.random.normal(rng, shape, jnp.float32)
    if pieces:
        entries = entries * level_of(rng, shape, pieces, -0.22, 0.18)
    return jnp.clip(entries, -reach, reach).astype(kind)


def setup_inputs(seed: int = 0) -> dict:
    streams_of = jax.random.split(jax.random.key(seed), 5)
    ancestor = bell_draw(streams_of[0], (ORDER, ORDER), 1.0, 6.0, ((0, 4), (1, 8)), jnp.float32)
    factor = bell_draw(streams_of[1], (2, ORDER, WIDTH), (LIST * TILE) ** -0.5, 0.0625, ((1, 32),), jnp.float32)
    diag_inverse = bell_draw(streams_of[2], (2, WIDTH, WIDTH), 1.0, 6.0, (), jnp.float32)
    structure = draw_structure(jax.random.fold_in(streams_of[4], 71), 0)
    return dict(ancestor=ancestor, factor=factor, diag_inverse=diag_inverse, structure=structure)


exact_mode = lax.Precision.HIGHEST


def reference(ancestor, factor, diag_inverse, structure):
    off_blocks = []
    diag_blocks = []
    for supernode in range(2):
        row_ids = (structure[supernode][:, None] * TILE + jnp.arange(TILE, dtype=jnp.int32)[None, :]).reshape(-1).astype(jnp.int32)
        sub_matrix = jnp.take(jnp.take(ancestor, row_ids, axis=0), row_ids, axis=1)
        sub_factor = jnp.take(factor[supernode], row_ids, axis=0)
        panel_rows = jnp.dot(sub_matrix, sub_factor, precision=exact_mode, preferred_element_type=jnp.float32)
        dense_rows = jnp.zeros((ORDER, WIDTH), jnp.float32).at[row_ids].set(panel_rows)
        off_blocks.append(-dense_rows)
        diag_blocks.append(diag_inverse[supernode] + jnp.dot(sub_factor.T, panel_rows, precision=exact_mode, preferred_element_type=jnp.float32))
    return jnp.stack(off_blocks), jnp.stack(diag_blocks)
```

```python
import functools

import jax
import jax.numpy as jnp
from jax import lax
from jax.experimental import pallas as pl
from jax.experimental.pallas import tpu as pltpu
from jax.sharding import PartitionSpec as P

TILE = 512


def tile_table(structure, tile_ids):
    hits = structure[:, :, None] == tile_ids[None, None, :]
    return jnp.any(hits, axis=1).astype(jnp.int32)


def product_kernel(rows, pieces, meta, a_ref, *refs):
    f_refs, out_ref, high, low = refs[:pieces], refs[pieces], refs[-2], refs[-1]
    step = pl.program_id(0)
    depth = high.shape[1]

    @pl.when(step == 0)
    def _():
        for q in range(pieces):
            whole = f_refs[q][...]
            top = whole.astype(jnp.bfloat16)
            high[q] = top
            low[q] = (whole - top.astype(jnp.float32)).astype(jnp.bfloat16)

    out_ref[...] = jnp.zeros_like(out_ref)

    @pl.when(meta[rows + step] > 0)
    def _():
        @pl.loop(0, pieces)
        def _(q):
            @pl.when(meta[2 * rows + q] > 0)
            def _():
                start = pl.multiple_of(meta[2 * rows + pieces + q] * depth, 128)
                part = a_ref[:, pl.ds(start, depth)]
                top = part.astype(jnp.bfloat16)
                rest = (part - top.astype(jnp.float32)).astype(jnp.bfloat16)
                dot = functools.partial(jnp.dot, preferred_element_type=jnp.float32)
                out_ref[0] += dot(top, high[q]) + (dot(top, low[q]) + dot(rest, high[q]))


def half_product(ancestor, pieces, row_flags, row_blocks, piece_flags, piece_places):
    rows, count = row_flags.shape[0], len(pieces)
    depth, width = pieces[0].shape
    fetch = jnp.maximum(lax.cummax(jnp.where(row_flags > 0, row_blocks, -1)), 0)
    meta = jnp.concatenate([fetch, row_flags, piece_flags, piece_places]).astype(jnp.int32)
    return pl.pallas_call(
        functools.partial(product_kernel, rows, count),
        out_shape=jax.ShapeDtypeStruct((rows, depth, width), jnp.float32),
        grid_spec=pltpu.PrefetchScalarGridSpec(
            num_scalar_prefetch=1,
            grid=(rows,),
            in_specs=[pl.BlockSpec((depth, ancestor.shape[1]), lambda i, m: (m[i], 0))]
            + [pl.BlockSpec((depth, width), lambda i, m: (0, 0))] * count,
            out_specs=pl.BlockSpec((1, depth, width), lambda i, m: (i, 0, 0)),
            scratch_shapes=[pltpu.VMEM((count, depth, width), jnp.bfloat16)] * 2,
        ),
        cost_estimate=pl.CostEstimate(
            flops=3 * rows * depth * ancestor.shape[1] * width,
            bytes_accessed=2 * rows * depth * ancestor.shape[1],
            transcendentals=0,
        ),
        compiler_params=pltpu.CompilerParams(vmem_limit_bytes=40 * 2**20),
    )(meta, ancestor, *pieces)


def per_device(ancestor, factor, diag_inverse, structure):
    z, c = lax.axis_index("row"), lax.axis_index("col")
    depth_z, width_c = lax.axis_size("row"), lax.axis_size("col")
    ratio = width_c // depth_z
    shard = factor.shape[1]
    col_bits = width_c.bit_length() - 1
    z_bits = depth_z.bit_length() - 1

    def across(value, bit):
        pairs = [(i, i ^ (1 << bit)) for i in range(width_c)]
        return lax.ppermute(value, "col", pairs)

    def gather_along_rows(own):
        up, down = [own], [own]
        for _ in range(depth_z - 1):
            up.append(lax.ppermute(up[-1], "row", [(i, i + 1) for i in range(depth_z - 1)]))
            down.append(lax.ppermute(down[-1], "row", [(i + 1, i) for i in range(depth_z - 1)]))
        slots = [own]
        for s in range(1, depth_z):
            slots.append(jnp.where(z >= s, up[s], down[depth_z - s]))
        return jnp.stack(slots)

    def to_columns(slots):
        got = []
        for q in range(depth_z):
            plane = (c % depth_z - q) % depth_z
            value = lax.dynamic_index_in_dim(slots, (z - plane) % depth_z, 0, keepdims=False)
            pairs = []
            for d in range(width_c):
                pairs.append(((d % ratio) * depth_z + (d // ratio + q) % depth_z, d))
            got.append(lax.ppermute(value, "col", pairs))
        return got

    def keep_and_send(value, bit, place):
        shape = value.shape
        split = value.reshape((-1, 2, 2**place) + shape[1:])
        mine = (c >> bit) & 1
        keep = lax.dynamic_index_in_dim(split, mine, 1, keepdims=False)
        send = lax.dynamic_index_in_dim(split, 1 - mine, 1, keepdims=False)
        return keep.reshape((-1,) + shape[1:]), send.reshape((-1,) + shape[1:])

    def scatter_rest(value, order):
        left = list(range(1, col_bits))
        for bit in order:
            keep, send = keep_and_send(value, bit, left.index(bit))
            left.remove(bit)
            value = keep + across(send, bit)
        return value[0]

    def sum_everywhere(value):
        for bit in range(col_bits):
            halves = value.reshape((2, -1) + value.shape[1:])
            mine = (c >> bit) & 1
            keep = lax.dynamic_index_in_dim(halves, mine, 0, keepdims=False)
            send = lax.dynamic_index_in_dim(halves, 1 - mine, 0, keepdims=False)
            value = keep + across(send, bit)
        for bit in range(z_bits):
            pairs = [(i, i ^ (1 << bit)) for i in range(depth_z)]
            value = value + lax.ppermute(value, "row", pairs)
        for bit in reversed(range(col_bits)):
            other = across(value, bit)
            odd = ((c >> bit) & 1) > 0
            value = jnp.concatenate([jnp.where(odd, other, value), jnp.where(odd, value, other)])
        return value

    core = c & 1
    halves = jnp.arange(width_c // 2, dtype=jnp.int32) * 2
    places = (c // ratio + jnp.arange(depth_z, dtype=jnp.int32)) % depth_z
    piece_tiles = (c * ancestor.shape[1] + places * shard) // TILE
    piece_table = tile_table(structure, piece_tiles)

    def rows_of(parity):
        blocks = halves + parity
        return blocks, tile_table(structure, (z * ancestor.shape[0] + blocks * shard) // TILE)

    keep_blocks, keep_table = rows_of(core)
    send_blocks, send_table = rows_of(1 - core)

    slots = [gather_along_rows(factor[k]) for k in range(2)]
    pieces = [to_columns(slots[k]) for k in range(2)]
    panels, diags = [], []
    for k in range(2):
        sent = half_product(ancestor, pieces[k], send_table[k], send_blocks, piece_table[k], places)
        arrived = across(sent, 0)
        kept = half_product(ancestor, pieces[k], keep_table[k], keep_blocks, piece_table[k], places)
        middle = kept.shape[2] // 2
        total = kept + arrived
        left = scatter_rest(total[:, :, :middle], range(1, col_bits))
        right = scatter_rest(total[:, :, middle:], reversed(range(1, col_bits)))
        panel = jnp.concatenate([left, right], axis=1)
        share = lax.dot_general(
            factor[k], panel, (((0,), (0,)), ((), ())),
            precision=lax.Precision.HIGHEST, preferred_element_type=jnp.float32,
        )
        panels.append(-panel)
        diags.append(diag_inverse[k] + sum_everywhere(share))
    return jnp.stack(panels), jnp.stack(diags)


def solution(mesh):
    in_specs = (P("row", "col"), P(None, ("row", "col"), None), P(), P())
    out_specs = (P(None, ("row", "col"), None), P())
    return jax.shard_map(
        per_device, mesh=mesh, in_specs=in_specs, out_specs=out_specs, check_vma=False
    )
```

```python
import functools

import jax
import jax.numpy as jnp
from jax import lax
from jax.experimental import pallas as pl
from jax.experimental.pallas import tpu as pltpu
from jax.sharding import PartitionSpec as P

TILE = 512


def tile_table(structure, tile_ids):
    hits = structure[:, :, None] == tile_ids[None, None, :]
    return jnp.any(hits, axis=1).astype(jnp.int32)


def product_kernel(rows, pieces, meta, a_ref, *refs):
    f_refs, out_ref, high, low = refs[:pieces], refs[pieces], refs[-2], refs[-1]
    step = pl.program_id(0)
    depth = high.shape[1]

    @pl.when(step == 0)
    def _():
        for q in range(pieces):
            whole = f_refs[q][...]
            top = whole.astype(jnp.bfloat16)
            high[q] = top
            low[q] = (whole - top.astype(jnp.float32)).astype(jnp.bfloat16)

    out_ref[...] = jnp.zeros_like(out_ref)

    @pl.when(meta[rows + step] > 0)
    def _():
        @pl.loop(0, pieces)
        def _(q):
            @pl.when(meta[2 * rows + q] > 0)
            def _():
                start = pl.multiple_of(meta[2 * rows + pieces + q] * depth, 128)
                part = a_ref[:, pl.ds(start, depth)]
                top = part.astype(jnp.bfloat16)
                rest = (part - top.astype(jnp.float32)).astype(jnp.bfloat16)
                dot = functools.partial(jnp.dot, preferred_element_type=jnp.float32)
                out_ref[0] += dot(top, high[q]) + (dot(top, low[q]) + dot(rest, high[q]))


def half_product(ancestor, pieces, row_flags, row_blocks, piece_flags, piece_places):
    rows, count = row_flags.shape[0], len(pieces)
    depth, width = pieces[0].shape
    fetch = jnp.maximum(lax.cummax(jnp.where(row_flags > 0, row_blocks, -1)), 0)
    meta = jnp.concatenate([fetch, row_flags, piece_flags, piece_places]).astype(jnp.int32)
    return pl.pallas_call(
        functools.partial(product_kernel, rows, count),
        out_shape=jax.ShapeDtypeStruct((rows, depth, width), jnp.float32),
        grid_spec=pltpu.PrefetchScalarGridSpec(
            num_scalar_prefetch=1,
            grid=(rows,),
            in_specs=[pl.BlockSpec((depth, ancestor.shape[1]), lambda i, m: (m[i], 0))]
            + [pl.BlockSpec((depth, width), lambda i, m: (0, 0))] * count,
            out_specs=pl.BlockSpec((1, depth, width), lambda i, m: (i, 0, 0)),
            scratch_shapes=[pltpu.VMEM((count, depth, width), jnp.bfloat16)] * 2,
        ),
        cost_estimate=pl.CostEstimate(
            flops=3 * rows * depth * ancestor.shape[1] * width,
            bytes_accessed=2 * rows * depth * ancestor.shape[1],
            transcendentals=0,
        ),
        compiler_params=pltpu.CompilerParams(vmem_limit_bytes=40 * 2**20),
    )(meta, ancestor, *pieces)


def per_device(ancestor, factor, diag_inverse, structure):
    z, c = lax.axis_index("row"), lax.axis_index("col")
    depth_z, width_c = lax.axis_size("row"), lax.axis_size("col")
    ratio = width_c // depth_z
    shard = factor.shape[1]
    col_bits = width_c.bit_length() - 1
    z_bits = depth_z.bit_length() - 1

    def across(value, bit):
        pairs = [(i, i ^ (1 << bit)) for i in range(width_c)]
        return lax.ppermute(value, "col", pairs)

    def gather_along_rows(own):
        up, down = [own], [own]
        for step in range(1, depth_z):
            rising = [(i, i + 1) for i in range(step - 1, depth_z - 1)]
            falling = [(i + 1, i) for i in range(depth_z - step)]
            up.append(lax.ppermute(up[-1], "row", rising))
            down.append(lax.ppermute(down[-1], "row", falling))
        slots = [own]
        for s in range(1, depth_z):
            slots.append(jnp.where(z >= s, up[s], down[depth_z - s]))
        return jnp.stack(slots), (up[depth_z - 2], down[depth_z - 2])

    def to_columns(slots):
        got = []
        for q in range(depth_z):
            plane = (c % depth_z - q) % depth_z
            value = lax.dynamic_index_in_dim(slots, (z - plane) % depth_z, 0, keepdims=False)
            pairs = []
            for d in range(width_c):
                pairs.append(((d % ratio) * depth_z + (d // ratio + q) % depth_z, d))
            got.append(lax.ppermute(value, "col", pairs))
        return got

    def keep_and_send(value, bit, place):
        shape = value.shape
        split = value.reshape((-1, 2, 2**place) + shape[1:])
        mine = (c >> bit) & 1
        keep = lax.dynamic_index_in_dim(split, mine, 1, keepdims=False)
        send = lax.dynamic_index_in_dim(split, 1 - mine, 1, keepdims=False)
        return keep.reshape((-1,) + shape[1:]), send.reshape((-1,) + shape[1:])

    def scatter_rest(value, order):
        left = list(range(1, col_bits))
        for bit in order:
            keep, send = keep_and_send(value, bit, left.index(bit))
            left.remove(bit)
            value = keep + across(send, bit)
        return value[0]

    def sum_everywhere(value):
        for bit in range(col_bits):
            halves = value.reshape((2, -1) + value.shape[1:])
            mine = (c >> bit) & 1
            keep = lax.dynamic_index_in_dim(halves, mine, 0, keepdims=False)
            send = lax.dynamic_index_in_dim(halves, 1 - mine, 0, keepdims=False)
            value = keep + across(send, bit)
        for bit in range(z_bits):
            pairs = [(i, i ^ (1 << bit)) for i in range(depth_z)]
            value = value + lax.ppermute(value, "row", pairs)
        for bit in reversed(range(col_bits)):
            other = across(value, bit)
            odd = ((c >> bit) & 1) > 0
            value = jnp.concatenate([jnp.where(odd, other, value), jnp.where(odd, value, other)])
        return value

    core = c & 1
    halves = jnp.arange(width_c // 2, dtype=jnp.int32) * 2
    places = (c // ratio + jnp.arange(depth_z, dtype=jnp.int32)) % depth_z
    piece_tiles = (c * ancestor.shape[1] + places * shard) // TILE
    piece_table = tile_table(structure, piece_tiles)

    def rows_of(parity):
        blocks = halves + parity
        return blocks, tile_table(structure, (z * ancestor.shape[0] + blocks * shard) // TILE)

    keep_blocks, keep_table = rows_of(core)
    send_blocks, send_table = rows_of(1 - core)

    def panel_of(k, pieces):
        sent = half_product(ancestor, pieces, send_table[k], send_blocks, piece_table[k], places)
        arrived = across(sent, 0)
        kept = half_product(ancestor, pieces, keep_table[k], keep_blocks, piece_table[k], places)
        middle = kept.shape[2] // 2
        left = scatter_rest(kept[:, :, :middle] + arrived[:, :, :middle], range(1, col_bits))
        right = scatter_rest(
            kept[:, :, middle:] + arrived[:, :, middle:], reversed(range(1, col_bits))
        )
        return jnp.concatenate([left, right], axis=1)

    def share_of(k, panel):
        return lax.dot_general(
            factor[k], panel, (((0,), (0,)), ((), ())),
            precision=lax.Precision.HIGHEST, preferred_element_type=jnp.float32,
        )

    half = factor.shape[2] // 2
    gate, panels = None, [[], []]
    for k in range(2):
        for start in (0, half):
            own = factor[k, :, start : start + half]
            if gate is not None:
                own, gate = lax.optimization_barrier((own, gate))
            slots, gate = gather_along_rows(own)
            panels[k].append(panel_of(k, to_columns(slots)))
    first = sum_everywhere(share_of(0, jnp.concatenate(panels[0], axis=1)))
    second = [sum_everywhere(share_of(1, part)) for part in panels[1]]
    panels = [jnp.concatenate(parts, axis=1) for parts in panels]
    sums = [first, jnp.concatenate(second, axis=1)]
    return -jnp.stack(panels), diag_inverse + jnp.stack(sums)


def solution(mesh):
    in_specs = (P("row", "col"), P(None, ("row", "col"), None), P(), P())
    out_specs = (P(None, ("row", "col"), None), P())
    return jax.shard_map(
        per_device, mesh=mesh, in_specs=in_specs, out_specs=out_specs, check_vma=False
    )
```
